128 devices in a mesh: group: 8 (over z_hi, y), row: 4 (over z_lo, core), col: 4 (over x).
Axes of the slice: x: 4, y: 4, z: 4 (z_hi: 2, z_lo: 2; z = z_hi * 2 + z_lo), core: 2. Of those that a mesh axis runs over, the one named last changes fastest.
Arguments:
- frontal: bfloat16 [8, 8192, 8192], P('group', 'row', 'col'), may hold values from -6 to 6
- panel_cols: bfloat16 [8, 8192, 384], P('group', ('row', 'col')), may hold values from -1.25 to 1.25
- inv_factor: bfloat16 [8, 384, 384], P('group'), as said below
- child_map: int32 [8, 64], replicated, may hold values from 0 to 63, as said below
- child_mask: int32 [8, 64], replicated, may hold values from 0 to 1, as said below
Outputs:
- assembled: bfloat16 [8, 8192, 8192], P('group', 'row', 'col')
The draws below stay inside these ranges and needn't reach their ends.
Inputs may be any that keep to these rules, and one draw needn't show every extreme that they name: `child_mask`: in each aligned run of 16 blocks exactly 8 blocks are live. `child_map`: the live blocks of one group map to distinct blocks; of the live blocks in one aligned run of 16 blocks exactly 2 map into each aligned run. A padding block maps to its own index. `inv_factor`: zero above the diagonal.
All inputs are finite; a program needn't handle non-finite values.
Results may differ from the reference program's by a relative error of at most 0.0053.
Values may be sent and summed in bfloat16 or wider, within the bound.
No kernel may reach another device: no remote copies, remote signals or barrier semaphores. Data moves between devices by JAX's collectives and lax.ppermute only.
A program may use at most 128 MiB of HBM per device.

```python
import jax
import jax.numpy as jnp
from jax import lax

M = 8192
P_SIZE = 384
BLK = 128
PAIR = 2
G = 8
NB = 64
BPR = 16
LIVE = 8


def block_plan(key):
    runs = NB // BPR

    def one_group(group_key):
        keys = jax.random.split(group_key, 4)
        run_ids = jnp.arange(runs, dtype=jnp.int32)
        live_pos = jax.vmap(lambda k: jax.random.permutation(k, BPR))(jax.random.split(keys[0], runs))[:, :LIVE].astype(jnp.int32)
        dest_perm = jax.vmap(lambda k: jax.random.permutation(k, LIVE))(jax.random.split(keys[1], runs)).astype(jnp.int32)
        slot_perm = jax.vmap(lambda k: jax.random.permutation(k, BPR))(jax.random.split(keys[2], runs)).astype(jnp.int32)
        arrive_perm = jax.vmap(lambda k: jax.random.permutation(k, LIVE))(jax.random.split(keys[3], runs)).astype(jnp.int32)
        dest_run = dest_perm // PAIR
        arrival = run_ids[:, None] * PAIR + dest_perm % PAIR
        slot = slot_perm[dest_run, arrive_perm[dest_run, arrival]]
        value = dest_run * BPR + slot
        source_ids = (run_ids[:, None] * BPR + live_pos).reshape(-1)
        targets = jnp.arange(NB, dtype=jnp.int32).at[source_ids].set(value.reshape(-1))
        live = jnp.zeros((NB,), jnp.int32).at[source_ids].set(1)
        return (targets, live)
    return jax.vmap(one_group)(jax.random.split(key, G))


def draw_child_map(key, part):
    return block_plan(key)[0]


def draw_child_mask(key, part):
    return block_plan(key)[1]


def draw_inv_factor(key, part):
    key = jax.random.fold_in(key, 7)
    key_diag, key_off = jax.random.split(key)
    lower = jnp.tril(jnp.ones((P_SIZE, P_SIZE), jnp.float32), -1)
    diag = jax.random.uniform(key_diag, (G, P_SIZE), jnp.float32, 0.6, 1.4)
    off = jax.random.normal(key_off, (G, P_SIZE, P_SIZE), jnp.float32) * (0.5 / P_SIZE ** 0.5)
    eye = jnp.eye(P_SIZE, dtype=jnp.float32)
    return (off * lower[None] + eye[None] * diag[:, :, None]).astype(jnp.bfloat16)


def shard_levels(key, shape, cuts, least, largest):
    factor_of, own = 1.0, jax.random.fold_in(key, 6)
    for position, parts in cuts:
        draws = jnp.exp(jax.random.uniform(jax.random.fold_in(own, position), (parts,), jnp.float32, least / len(cuts), largest / len(cuts)))
        factor_of = factor_of * jnp.repeat(draws, shape[position] // parts).reshape([-1 if axis == position else 1 for axis in range(len(shape))])
    return factor_of


def centred(stream_key, extent, width, bound, pieces=(), kind=jnp.bfloat16):
    entries = jax.random.normal(stream_key, extent, jnp.float32) * width
    if len(pieces) > 0:
        entries = shard_levels(stream_key, extent, pieces, -0.22, 0.18) * entries
    return jnp.clip(entries, min=-bound, max=bound).astype(kind)


def setup_inputs(seed: int = 0) -> dict:
    arg_keys = jax.random.split(jax.random.key(seed), 6)
    frontal = centred(arg_keys[0], (G, M, M), 1.0, 6.0, ((0, 8), (1, 4), (2, 4)))
    panel_cols = centred(arg_keys[1], (G, M, P_SIZE), 20 ** -0.5, 1.25, ((0, 8), (1, 16)))
    inv_factor = draw_inv_factor(jax.random.fold_in(arg_keys[5], 71), 0)
    child_map = draw_child_map(jax.random.fold_in(arg_keys[5], 71), 0)
    child_mask = draw_child_mask(jax.random.fold_in(arg_keys[5], 71), 0)
    return dict(frontal=frontal, panel_cols=panel_cols, inv_factor=inv_factor, child_map=child_map, child_mask=child_mask)


def one_group(front_g, panel_g, inv_g):
    factor = jnp.dot(panel_g, inv_g.T, preferred_element_type=jnp.float32).astype(jnp.bfloat16)
    return front_g.astype(jnp.float32) - jnp.dot(factor, factor.T, preferred_element_type=jnp.float32)


def incoming(targets, live, carried):
    block_ids = jnp.arange(NB, dtype=jnp.int32)
    hits = (targets[:, None] == block_ids[None, :]) & (live[:, None] == 1)
    source = jnp.sum(jnp.where(hits, block_ids[:, None], 0), axis=0).astype(jnp.int32)
    present = jnp.any(hits, axis=0).astype(jnp.float32)
    blocks = carried.reshape(NB, BLK, NB, BLK)
    picked = jnp.take(jnp.take(blocks, source, axis=0), source, axis=2).astype(jnp.float32)
    weight = present[:, None, None, None] * present[None, None, :, None]
    return (picked * weight).reshape(M, M)


def reference(frontal, panel_cols, inv_factor, child_map, child_mask):
    total = frontal.shape[0]

    def step(carry, index):
        below, has_child = carry
        upd = one_group(lax.dynamic_index_in_dim(frontal, index, 0, False), lax.dynamic_index_in_dim(panel_cols, index, 0, False), lax.dynamic_index_in_dim(inv_factor, index, 0, False))
        child = jnp.minimum(index + 1, total - 1).astype(jnp.int32)
        targets = lax.dynamic_index_in_dim(child_map, child, 0, False)
        live = lax.dynamic_index_in_dim(child_mask, child, 0, False)
        placed = incoming(targets, live, below)
        result = (upd + has_child * placed).astype(jnp.bfloat16)
        return (upd.astype(jnp.bfloat16), jnp.ones((), jnp.float32)), result

    start = (jnp.zeros((M, M), jnp.bfloat16), jnp.zeros((), jnp.float32))
    _, outputs = lax.scan(step, start, jnp.arange(total, dtype=jnp.int32), reverse=True)
    return outputs
```

```python
import functools

import jax
import jax.numpy as jnp
from jax import lax
from jax.experimental import pallas as pl
from jax.experimental.pallas import tpu as pltpu
from jax.sharding import PartitionSpec as P

BLK = 128
AXES = ("group", "row", "col")
ANY = pl.BlockSpec(memory_space=pl.ANY)
SMEM = pl.BlockSpec(memory_space=pltpu.SMEM)
VMEM = pl.BlockSpec(memory_space=pltpu.VMEM)
DEPTH = (((1,), (1,)), ((), ()))


def params(mib):
    return pltpu.CompilerParams(vmem_limit_bytes=mib << 20)


def move(array, target):
    groups, rows, cols = (lax.axis_size(axis) for axis in AXES)
    pairs = []
    for g in range(groups):
        for r in range(rows):
            for c in range(cols):
                tg, tr, tc = target(g, r, c)
                if tg >= 0:
                    pairs.append(((g * rows + r) * cols + c, (tg * rows + tr) * cols + tc))
    return lax.ppermute(array, AXES, pairs)


def plan_kernel(map_ref, mask_ref, out_ref):
    count = map_ref.shape[1]
    runs = lax.axis_size("row")
    span = count // runs
    group = lax.axis_index("group")
    child = jnp.minimum(group + 1, map_ref.shape[0] - 1)

    def coded(g, run):
        out = []
        for k in range(span):
            target = map_ref[g, run * span + k]
            live = mask_ref[g, run * span + k] == 1
            out.append((jnp.where(live, target // span, -1), target * span + k))
        return out

    def ends(codes, run):
        low, high = jnp.int32(1 << 20), jnp.int32(-1)
        for to, code in codes:
            hit = to == run
            low = jnp.minimum(low, jnp.where(hit, code, 1 << 20))
            high = jnp.maximum(high, jnp.where(hit, code, -1))
        return low, high

    for position, axis in enumerate(("row", "col")):
        me = lax.axis_index(axis)
        own = coded(group, me)
        for run in range(runs):
            for i, code in enumerate(ends(own, run)):
                out_ref[position * 2 * runs + 2 * run + i] = lax.rem(code, span)
        for d in range(runs):
            for i, code in enumerate(ends(coded(child, me ^ d), me)):
                out_ref[(position + 2) * 2 * runs + 2 * d + i] = code // span - me * span


def plan(child_map, child_mask):
    return pl.pallas_call(
        plan_kernel,
        out_shape=jax.ShapeDtypeStruct((32,), jnp.int32),
        in_specs=[SMEM, SMEM],
        out_specs=SMEM,
        name="plan",
    )(child_map, child_mask)


def load_factor(shards, rows_v, cols_v, sems):
    size = shards[0].shape[0]
    copies = []
    for axis, held, refs in (("col", rows_v, shards[:4]), ("row", cols_v, shards[4:])):
        me = lax.axis_index(axis)
        for d, ref in enumerate(refs):
            copies.append(
                pltpu.make_async_copy(ref, held.at[pl.ds((me ^ d) * size, size)], sems.at[len(copies)])
            )
    for copy in copies:
        copy.start()
    return copies


def picked_kernel(sending, idx, *refs):
    shards, frontal = refs[:8], refs[8]
    outs = refs[9:13]
    rows_v, cols_v, front_v, pick_v, sems = refs[13:]
    row, col = lax.axis_index("row"), lax.axis_index("col")
    copies = load_factor(shards, rows_v, cols_v, sems)
    row_at, col_at = [], []
    for d in range(4):
        for i in range(2):
            if sending:
                row_at.append(idx[2 * (row ^ d) + i])
                col_at.append(idx[8 + 2 * (col ^ d) + i])
            else:
                row_at.append(idx[16 + 2 * d + i])
                col_at.append(idx[24 + 2 * d + i])
    for a in range(8):
        for b in range(8):
            pltpu.make_async_copy(
                frontal.at[
                    pl.ds(pl.multiple_of(row_at[a] * BLK, BLK), BLK),
                    pl.ds(pl.multiple_of(col_at[b] * BLK, BLK), BLK),
                ],
                front_v.at[a * 8 + b],
                sems.at[8],
            ).start()
    for copy in copies:
        copy.wait()
    for b in range(8):
        pick_v[b * BLK : (b + 1) * BLK, :] = cols_v[pl.ds(pl.multiple_of(col_at[b] * BLK, BLK), BLK), :]
    pltpu.make_async_copy(front_v, front_v, sems.at[8]).wait()
    for d in range(4):
        left = jnp.concatenate(
            [rows_v[pl.ds(pl.multiple_of(row_at[2 * d + i] * BLK, BLK), BLK), :] for i in range(2)], axis=0
        )
        product = lax.dot_general(left, pick_v[...], DEPTH, preferred_element_type=jnp.float32)
        for e in range(4):
            for i in range(2):
                for j in range(2):
                    at = ((e * 2 + i) * 2 + j) * BLK
                    b = 2 * e + j
                    value = front_v[(2 * d + i) * 8 + b].astype(jnp.float32)
                    value = value - product[i * BLK : (i + 1) * BLK, b * BLK : (b + 1) * BLK]
                    outs[d][at : at + BLK, :] = value.astype(outs[d].dtype)


def picked(idx, shards, frontal, sending):
    dtype = jnp.bfloat16 if sending else jnp.float32
    depth = shards[0].shape[1]
    return pl.pallas_call(
        functools.partial(picked_kernel, sending),
        out_shape=[jax.ShapeDtypeStruct((16 * BLK, BLK), dtype)] * 4,
        in_specs=[SMEM] + [ANY] * 9,
        out_specs=[VMEM] * 4,
        scratch_shapes=[
            pltpu.VMEM((frontal.shape[0], depth), jnp.bfloat16),
            pltpu.VMEM((frontal.shape[1], depth), jnp.bfloat16),
            pltpu.VMEM((64, BLK, BLK), jnp.bfloat16),
            pltpu.VMEM((8 * BLK, depth), jnp.bfloat16),
            pltpu.SemaphoreType.DMA((9,)),
        ],
        compiler_params=params(40),
        cost_estimate=pl.CostEstimate(flops=2 * 1024 * 1024 * 384, bytes_accessed=10 << 20, transcendentals=0),
        name="picked_send" if sending else "picked_own",
    )(idx, *shards, frontal)


def update_kernel(frontal, *refs):
    shards, out = refs[:8], refs[8]
    rows_v, cols_v, sems = refs[9:]
    step = pl.program_id(0)

    @pl.when(step == 0)
    def _():
        for copy in load_factor(shards, rows_v, cols_v, sems):
            copy.wait()

    high, wide = out.shape
    across = cols_v.shape[0] // wide
    left = rows_v[pl.ds(pl.multiple_of(step // across * high, high), high), :]
    right = cols_v[pl.ds(pl.multiple_of(lax.rem(step, across) * wide, wide), wide), :]
    product = lax.dot_general(left, right, DEPTH, preferred_element_type=jnp.float32)
    out[...] = (frontal[...].astype(jnp.float32) - product).astype(jnp.bfloat16)


def updated(shards, frontal):
    tile, depth = frontal.shape[0], shards[0].shape[1]
    high, wide = 512, 1024
    across = tile // wide
    block = pl.BlockSpec((high, wide), lambda s: (s // across, s % across))
    return pl.pallas_call(
        update_kernel,
        out_shape=jax.ShapeDtypeStruct((tile, tile), jnp.bfloat16),
        grid=(tile // high * across,),
        in_specs=[block] + [ANY] * 8,
        out_specs=block,
        scratch_shapes=[
            pltpu.VMEM((tile, depth), jnp.bfloat16),
            pltpu.VMEM((tile, depth), jnp.bfloat16),
            pltpu.SemaphoreType.DMA((8,)),
        ],
        compiler_params=params(40),
        cost_estimate=pl.CostEstimate(flops=2 * tile * tile * depth, bytes_accessed=20 << 20, transcendentals=0),
        name="update",
    )(frontal, *shards)


def place_kernel(d, idx, own, here, x1, x2, x3, _, out, block_v, sem):
    copies = []
    for e, ref in enumerate((here, x1, x2, x3)):
        for i in range(2):
            for j in range(2):
                k = (e * 2 + i) * 2 + j
                at = (i * 2 + j) * BLK
                block_v[k] = (own[k * BLK : (k + 1) * BLK, :] + ref[at : at + BLK, :].astype(jnp.float32)).astype(
                    jnp.bfloat16
                )
                pltpu.make_async_copy(
                    block_v.at[k],
                    out.at[
                        pl.ds(pl.multiple_of(idx[16 + 2 * d + i] * BLK, BLK), BLK),
                        pl.ds(pl.multiple_of(idx[24 + 2 * e + j] * BLK, BLK), BLK),
                    ],
                    sem,
                ).start()
    pltpu.make_async_copy(block_v, block_v, sem).wait()


def placed(idx, d, own, here, others, out):
    quarter = pl.BlockSpec((4 * BLK, BLK), lambda s: (0, 0))
    whole = pl.BlockSpec((16 * BLK, BLK), lambda s: (0, 0))
    return pl.pallas_call(
        functools.partial(place_kernel, d),
        out_shape=jax.ShapeDtypeStruct(out.shape, out.dtype),
        grid=(1,),
        in_specs=[SMEM, whole, quarter, quarter, quarter, quarter, ANY],
        out_specs=ANY,
        scratch_shapes=[pltpu.VMEM((16, BLK, BLK), jnp.bfloat16), pltpu.SemaphoreType.DMA],
        input_output_aliases={6: 0},
        compiler_params=params(16),
        cost_estimate=pl.CostEstimate(flops=1 << 18, bytes_accessed=2 << 20, transcendentals=0),
        name="place",
    )(idx, own, here, *others, out)


def on_device(frontal, panel_cols, inv_factor, child_map, child_mask):
    front = frontal[0]
    idx = plan(child_map, child_mask)
    factor = lax.dot_general(panel_cols[0], inv_factor[0], DEPTH, preferred_element_type=jnp.float32).astype(
        jnp.bfloat16
    )
    turned = move(factor, lambda g, r, c: (g, c, r))
    by_col = [factor] + [move(factor, lambda g, r, c, d=d: (g, r, c ^ d)) for d in (1, 2, 3)]
    far = move(turned, lambda g, r, c: (g, r ^ 2, c))
    by_row = [turned, move(turned, lambda g, r, c: (g, r ^ 1, c)), far, move(far, lambda g, r, c: (g, r ^ 1, c))]
    shards = by_col + by_row
    sent = picked(idx, shards, front, True)
    came = [move(sent[d], lambda g, r, c, d=d: (g - 1, r ^ d, c)) for d in range(4)]
    out = updated(shards, front)
    own = picked(idx, shards, front, False)
    quarter = 4 * BLK
    for d in range(4):
        others = [
            move(came[d][e * quarter : (e + 1) * quarter], lambda g, r, c, e=e: (g, r, c ^ e)) for e in (1, 2, 3)
        ]
        out = placed(idx, d, own[d], came[d], others, out)
    return out[None]


def solution(mesh):
    specs = (
        P("group", "row", "col"),
        P("group", ("row", "col"), None),
        P("group", None, None),
        P(),
        P(),
    )
    return jax.shard_map(
        on_device, mesh=mesh, in_specs=specs, out_specs=P("group", "row", "col"), check_vma=False
    )
```

```python
import functools

import jax
import jax.numpy as jnp
from jax import lax
from jax.experimental import pallas as pl
from jax.experimental.pallas import tpu as pltpu
from jax.sharding import PartitionSpec as P

BLK = 128
AXES = ("group", "row", "col")
ANY = pl.BlockSpec(memory_space=pl.ANY)
SMEM = pl.BlockSpec(memory_space=pltpu.SMEM)
VMEM = pl.BlockSpec(memory_space=pltpu.VMEM)
DEPTH = (((1,), (1,)), ((), ()))


def params(mib):
    return pltpu.CompilerParams(vmem_limit_bytes=mib << 20)


def move(array, target):
    groups, rows, cols = (lax.axis_size(axis) for axis in AXES)
    pairs = []
    for g in range(groups):
        for r in range(rows):
            for c in range(cols):
                to = target(g, r, c)
                if to is not None and to[0] >= 0:
                    tg, tr, tc = to
                    pairs.append(((g * rows + r) * cols + c, (tg * rows + tr) * cols + tc))
    return lax.ppermute(array, AXES, pairs)


def codes(map_ref, mask_ref, group, run, span):
    out = []
    for k in range(span):
        target = map_ref[group, run * span + k]
        live = mask_ref[group, run * span + k] == 1
        out.append((jnp.where(live, target // span, -1), target * span + k))
    return out


def ends(coded, run):
    low, high = jnp.int32(1 << 20), jnp.int32(-1)
    for to, code in coded:
        hit = to == run
        low = jnp.minimum(low, jnp.where(hit, code, 1 << 20))
        high = jnp.maximum(high, jnp.where(hit, code, -1))
    return low, high


def plan_kernel(map_ref, mask_ref, out_ref):
    count = map_ref.shape[1]
    runs = lax.axis_size("row")
    span = count // runs
    group = lax.axis_index("group")
    child = jnp.minimum(group + 1, map_ref.shape[0] - 1)
    for position, axis in enumerate(("row", "col")):
        me = lax.axis_index(axis)
        own = codes(map_ref, mask_ref, group, me, span)
        for run in range(runs):
            for i, code in enumerate(ends(own, run)):
                out_ref[position * 2 * runs + 2 * run + i] = lax.rem(code, span)
        for d in range(runs):
            for i, code in enumerate(ends(codes(map_ref, mask_ref, child, me ^ d, span), me)):
                out_ref[(position + 2) * 2 * runs + 2 * d + i] = code // span - me * span


def plan(child_map, child_mask):
    return pl.pallas_call(
        plan_kernel,
        out_shape=jax.ShapeDtypeStruct((32,), jnp.int32),
        in_specs=[SMEM, SMEM],
        out_specs=SMEM,
        compiler_params=params(16),
        name="plan",
    )(child_map, child_mask)


def load_factor(shards, rows_v, cols_v):
    size = shards[0].shape[0]
    half = size // 2
    row, col = lax.axis_index("row"), lax.axis_index("col")
    alike = lax.rem(row + col, 2) == 0
    places = [((col ^ d) * size, size) for d in (0, 1, 3)] + [((col ^ 2) * size + n * half, half) for n in range(2)]
    for ref, (start, count) in zip(shards[:5], places):
        rows_v[pl.ds(pl.multiple_of(start, half), count), :] = ref[...]
    for d in range(4):
        place = pl.ds(pl.multiple_of((col ^ d) * size, size), size)

        @pl.when(alike)
        def _():
            cols_v[place, :] = shards[5 + 2 * d][...]

        @pl.when(jnp.logical_not(alike))
        def _():
            cols_v[place, :] = shards[6 + 2 * d][...]


def pack_kernel(idx, frontal, out, sem):
    row, col = lax.axis_index("row"), lax.axis_index("col")
    row_at = [pl.multiple_of(idx[2 * (row ^ d) + i] * BLK, BLK) for d in range(4) for i in range(2)]
    col_at = [pl.multiple_of(idx[8 + 2 * (col ^ e) + j] * BLK, BLK) for e in range(4) for j in range(2)]
    for a in range(8):
        for b in range(8):
            pltpu.make_async_copy(
                frontal.at[pl.ds(row_at[a], BLK), pl.ds(col_at[b], BLK)], out.at[a * 8 + b], sem
            ).start()
    pltpu.make_async_copy(out, out, sem).wait()


def pack(idx, frontal):
    return pl.pallas_call(
        pack_kernel,
        out_shape=jax.ShapeDtypeStruct((64, BLK, BLK), frontal.dtype),
        in_specs=[SMEM, ANY],
        out_specs=VMEM,
        scratch_shapes=[pltpu.SemaphoreType.DMA],
        compiler_params=params(16),
        cost_estimate=pl.CostEstimate(flops=0, bytes_accessed=4 << 20, transcendentals=0),
        name="pack",
    )(idx, frontal)


def picked_kernel(idx, *refs):
    shards, packed = refs[:13], refs[13]
    outs = refs[14:21]
    rows_v, cols_v, pick_v = refs[21:]
    row, col = lax.axis_index("row"), lax.axis_index("col")
    load_factor(shards, rows_v, cols_v)
    row_at = [pl.multiple_of(idx[2 * (row ^ d) + i] * BLK, BLK) for d in range(4) for i in range(2)]
    col_at = [pl.multiple_of(idx[8 + 2 * (col ^ e) + j] * BLK, BLK) for e in range(4) for j in range(2)]
    for b in range(8):
        pick_v[b * BLK : (b + 1) * BLK, :] = cols_v[pl.ds(col_at[b], BLK), :]
    for d in range(4):
        left = jnp.concatenate([rows_v[pl.ds(row_at[2 * d + i], BLK), :] for i in range(2)], axis=0)
        product = lax.dot_general(left, pick_v[...], DEPTH, preferred_element_type=jnp.float32)
        for e in range(4):
            for i in range(2):
                for j in range(2):
                    b = 2 * e + j
                    value = packed[(2 * d + i) * 8 + b].astype(jnp.float32)
                    value = value - product[i * BLK : (i + 1) * BLK, b * BLK : (b + 1) * BLK]
                    if d < 3:
                        ref, at = outs[d], (e * 2 + i) * 2 + j
                    else:
                        ref, at = outs[3 + e], i * 2 + j
                    ref[at * BLK : (at + 1) * BLK, :] = value.astype(jnp.bfloat16)


def picked(idx, shards, packed):
    size, depth = shards[0].shape
    return pl.pallas_call(
        picked_kernel,
        out_shape=[jax.ShapeDtypeStruct((blocks * BLK, BLK), jnp.bfloat16) for blocks in (16, 16, 16, 4, 4, 4, 4)],
        in_specs=[SMEM] + [VMEM] * 14,
        out_specs=[VMEM] * 7,
        scratch_shapes=[
            pltpu.VMEM((4 * size, depth), jnp.bfloat16),
            pltpu.VMEM((4 * size, depth), jnp.bfloat16),
            pltpu.VMEM((8 * BLK, depth), jnp.bfloat16),
        ],
        compiler_params=params(24),
        cost_estimate=pl.CostEstimate(flops=2 * 1024 * 1024 * 384, bytes_accessed=8 << 20, transcendentals=0),
        name="picked",
    )(idx, *shards, packed)


def update_kernel(idx, frontal, *refs):
    shards, out, owns = refs[:13], refs[13], refs[14:18]
    rows_v, cols_v, whole_v = refs[18:]
    step = pl.program_id(0)

    @pl.when(step == 0)
    def _():
        load_factor(shards, rows_v, cols_v)

    high = out.shape[0]
    left = rows_v[pl.ds(pl.multiple_of(step * high, high), high), :]
    product = lax.dot_general(left, cols_v[...], DEPTH, preferred_element_type=jnp.float32)
    value = frontal[...].astype(jnp.float32) - product
    out[...] = value.astype(jnp.bfloat16)
    whole_v[...] = value
    per = high // BLK
    for d in range(4):
        for i in range(2):
            at = idx[16 + 2 * d + i]

            @pl.when(at // per == step)
            def _():
                strip = pl.ds(pl.multiple_of(lax.rem(at, per) * BLK, BLK), BLK)
                for e in range(4):
                    for j in range(2):
                        k = ((e * 2 + i) * 2 + j) * BLK
                        wide = pl.ds(pl.multiple_of(idx[24 + 2 * e + j] * BLK, BLK), BLK)
                        owns[d][k : k + BLK, :] = whole_v[strip, wide]


def updated(idx, shards, frontal):
    tile, depth = frontal.shape[0], shards[0].shape[1]
    high = 512
    block = pl.BlockSpec((high, tile), lambda s: (s, 0))
    return pl.pallas_call(
        update_kernel,
        out_shape=[jax.ShapeDtypeStruct((tile, tile), jnp.bfloat16)]
        + [jax.ShapeDtypeStruct((16 * BLK, BLK), jnp.float32)] * 4,
        grid=(tile // high,),
        in_specs=[SMEM, block] + [VMEM] * 13,
        out_specs=[block] + [VMEM] * 4,
        scratch_shapes=[
            pltpu.VMEM((tile, depth), jnp.bfloat16),
            pltpu.VMEM((tile, depth), jnp.bfloat16),
            pltpu.VMEM((high, tile), jnp.float32),
        ],
        compiler_params=params(40),
        cost_estimate=pl.CostEstimate(flops=2 * tile * tile * depth, bytes_accessed=24 << 20, transcendentals=0),
        name="update",
    )(idx, frontal, *shards)


def place_kernel(first, count, split, idx, *refs):
    owns, parts = refs[:count], refs[count : count + split]
    out, block_v, sem = refs[count + split + 1 :]
    for n in range(count):
        for e in range(4):
            for i in range(2):
                for j in range(2):
                    k = (e * 2 + i) * 2 + j
                    if split == count:
                        ref, at = parts[n], k
                    elif e == 0:
                        ref, at = parts[n], i * 2 + j
                    else:
                        ref, at = parts[count + e - 1], (n * 2 + i) * 2 + j
                    value = owns[n][k * BLK : (k + 1) * BLK, :]
                    value = value + ref[at * BLK : (at + 1) * BLK, :].astype(jnp.float32)
                    block_v[n * 16 + k] = value.astype(jnp.bfloat16)
                    pltpu.make_async_copy(
                        block_v.at[n * 16 + k],
                        out.at[
                            pl.ds(pl.multiple_of(idx[16 + 2 * (first + n) + i] * BLK, BLK), BLK),
                            pl.ds(pl.multiple_of(idx[24 + 2 * e + j] * BLK, BLK), BLK),
                        ],
                        sem,
                    ).start()
    pltpu.make_async_copy(block_v, block_v, sem).wait()


def placed(idx, first, own, parts, out):
    count, split = len(own), len(parts)

    return pl.pallas_call(
        functools.partial(place_kernel, first, count, split),
        out_shape=jax.ShapeDtypeStruct(out.shape, out.dtype),
        in_specs=[SMEM] + [VMEM] * (count + split) + [ANY],
        out_specs=ANY,
        scratch_shapes=[pltpu.VMEM((16 * count, BLK, BLK), jnp.bfloat16), pltpu.SemaphoreType.DMA],
        input_output_aliases={count + split + 1: 0},
        compiler_params=params(12),
        cost_estimate=pl.CostEstimate(flops=1 << 18, bytes_accessed=count << 21, transcendentals=0),
        name="place",
    )(idx, *own, *parts, out)


def after(array, *done):
    return lax.optimization_barrier((array, *done))[0]


def on_device(frontal, panel_cols, inv_factor, child_map, child_mask):
    front = frontal[0]
    quarter = 4 * BLK

    def hop(d, array):
        return move(array, lambda g, r, c: (g - 1, r ^ d, c))

    def flip_row(d, array):
        return move(array, lambda g, r, c: (g, r ^ d, c))

    def flip_col(d, array):
        return move(array, lambda g, r, c: (g, r, c ^ d))

    factor = lax.dot_general(panel_cols[0], inv_factor[0], DEPTH, preferred_element_type=jnp.float32).astype(
        jnp.bfloat16
    )
    across = flip_row(2, factor)
    near = [flip_col(1, factor), flip_col(3, factor)]
    idx = plan(child_map, child_mask)
    packed = pack(idx, front)
    row, col = lax.axis_index("row"), lax.axis_index("col")
    same = row // 2 == col // 2
    alike = (row + col) % 2 == 0
    across = after(across, packed, *near)
    low, high = jnp.where(same, factor, across), jnp.where(same, across, factor)
    half = factor.shape[0] // 2
    by_col = [factor, *near, flip_col(1, near[1][:half]), flip_col(3, near[0][half:])]
    third = move(high, lambda g, r, c: (g, r, c ^ 3) if (r + c) % 2 else None)
    one = move(
        jnp.where(alike, high, low), lambda g, r, c: (g, r ^ 1, c ^ 1) if (r + c) % 2 else (g, r, c ^ 2)
    )

    def swap(array):
        return move(array, lambda g, r, c: None if (r + c) % 2 else (g, r ^ 1, c))

    other = flip_row(1, after(one, *by_col[3:]))
    shards = by_col + [low, swap(low), other, one, one, other, third, swap(after(third, *by_col[3:]))]
    sent = picked(idx, shards, packed)
    came = [hop(d, sent[d]) for d in range(3)]
    crossed = [sent[3]] + [flip_col(e, sent[3 + e]) for e in (1, 2, 3)]
    came.append(hop(3, jnp.concatenate(crossed)))
    out, *own = updated(idx, shards, after(front, came[0]))
    for changes in ((0, 1), (2,)):
        parts = [came[d] for d in changes]
        for e in (1, 2, 3):
            blocks = [came[d][e * quarter : (e + 1) * quarter] for d in changes]
            blocks = jnp.concatenate(blocks) if len(blocks) > 1 else blocks[0]
            parts.append(flip_col(e, after(blocks, own[0])))
        out = placed(idx, changes[0], [own[d] for d in changes], parts, out)
    return placed(idx, 3, own[3:], came[3:], out)[None]


def solution(mesh):
    specs = (
        P("group", "row", "col"),
        P("group", ("row", "col"), None),
        P("group", None, None),
        P(),
        P(),
    )
    return jax.shard_map(
        on_device, mesh=mesh, in_specs=specs, out_specs=P("group", "row", "col"), check_vma=False
    )
```

```python
import functools

import jax
import jax.numpy as jnp
from jax import lax
from jax.experimental import pallas as pl
from jax.experimental.pallas import tpu as pltpu
from jax.sharding import PartitionSpec as P

BLK = 128
AXES = ("group", "row", "col")
ANY = pl.BlockSpec(memory_space=pl.ANY)
SMEM = pl.BlockSpec(memory_space=pltpu.SMEM)
VMEM = pl.BlockSpec(memory_space=pltpu.VMEM)
DEPTH = (((1,), (1,)), ((), ()))


def params(mib):
    return pltpu.CompilerParams(vmem_limit_bytes=mib << 20)


def move(array, target):
    groups, rows, cols = (lax.axis_size(axis) for axis in AXES)
    pairs = []
    for g in range(groups):
        for r in range(rows):
            for c in range(cols):
                to = target(g, r, c)
                if to is not None and to[0] >= 0:
                    tg, tr, tc = to
                    pairs.append(((g * rows + r) * cols + c, (tg * rows + tr) * cols + tc))
    return lax.ppermute(array, AXES, pairs)


def codes(map_ref, mask_ref, group, run, span):
    out = []
    for k in range(span):
        target = map_ref[group, run * span + k]
        live = mask_ref[group, run * span + k] == 1
        out.append((jnp.where(live, target // span, -1), target * span + k))
    return out


def ends(coded, run):
    low, high = jnp.int32(1 << 20), jnp.int32(-1)
    for to, code in coded:
        hit = to == run
        low = jnp.minimum(low, jnp.where(hit, code, 1 << 20))
        high = jnp.maximum(high, jnp.where(hit, code, -1))
    return low, high


def plan_kernel(map_ref, mask_ref, out_ref):
    count = map_ref.shape[1]
    runs = lax.axis_size("row")
    span = count // runs
    group = lax.axis_index("group")
    child = jnp.minimum(group + 1, map_ref.shape[0] - 1)
    for position, axis in enumerate(("row", "col")):
        me = lax.axis_index(axis)
        own = codes(map_ref, mask_ref, group, me, span)
        for run in range(runs):
            for i, code in enumerate(ends(own, run)):
                out_ref[position * 2 * runs + 2 * run + i] = lax.rem(code, span)
        for d in range(runs):
            for i, code in enumerate(ends(codes(map_ref, mask_ref, child, me ^ d, span), me)):
                out_ref[(position + 2) * 2 * runs + 2 * d + i] = code // span - me * span


def plan(child_map, child_mask):
    return pl.pallas_call(
        plan_kernel,
        out_shape=jax.ShapeDtypeStruct((32,), jnp.int32),
        in_specs=[SMEM, SMEM],
        out_specs=SMEM,
        compiler_params=params(16),
        name="plan",
    )(child_map, child_mask)


def load_factor(shards, rows_v, cols_v):
    size = shards[0].shape[0]
    half = size // 2
    row, col = lax.axis_index("row"), lax.axis_index("col")
    alike = lax.rem(row + col, 2) == 0
    places = [((col ^ d) * size, size) for d in (0, 1, 3)] + [((col ^ 2) * size + n * half, half) for n in range(2)]
    for ref, (start, count) in zip(shards[:5], places):
        rows_v[pl.ds(pl.multiple_of(start, half), count), :] = ref[...]
    for d in range(4):
        place = pl.ds(pl.multiple_of((col ^ d) * size, size), size)

        @pl.when(alike)
        def _():
            cols_v[place, :] = shards[5 + 2 * d][...]

        @pl.when(jnp.logical_not(alike))
        def _():
            cols_v[place, :] = shards[6 + 2 * d][...]


def pack_kernel(idx, frontal, out, sem):
    row, col = lax.axis_index("row"), lax.axis_index("col")
    row_at = [pl.multiple_of(idx[2 * (row ^ d) + i] * BLK, BLK) for d in range(4) for i in range(2)]
    col_at = [pl.multiple_of(idx[8 + 2 * (col ^ e) + j] * BLK, BLK) for e in range(4) for j in range(2)]
    for a in range(8):
        for b in range(8):
            pltpu.make_async_copy(
                frontal.at[pl.ds(row_at[a], BLK), pl.ds(col_at[b], BLK)], out.at[a * 8 + b], sem
            ).start()
    pltpu.make_async_copy(out, out, sem).wait()


def pack(idx, frontal):
    return pl.pallas_call(
        pack_kernel,
        out_shape=jax.ShapeDtypeStruct((64, BLK, BLK), frontal.dtype),
        in_specs=[SMEM, ANY],
        out_specs=VMEM,
        scratch_shapes=[pltpu.SemaphoreType.DMA],
        compiler_params=params(16),
        cost_estimate=pl.CostEstimate(flops=0, bytes_accessed=4 << 20, transcendentals=0),
        name="pack",
    )(idx, frontal)


def picked_kernel(idx, *refs):
    shards, packed = refs[:13], refs[13]
    outs = refs[14:21]
    rows_v, cols_v, pick_v = refs[21:]
    row, col = lax.axis_index("row"), lax.axis_index("col")
    load_factor(shards, rows_v, cols_v)
    row_at = [pl.multiple_of(idx[2 * (row ^ d) + i] * BLK, BLK) for d in range(4) for i in range(2)]
    col_at = [pl.multiple_of(idx[8 + 2 * (col ^ e) + j] * BLK, BLK) for e in range(4) for j in range(2)]
    for b in range(8):
        pick_v[b * BLK : (b + 1) * BLK, :] = cols_v[pl.ds(col_at[b], BLK), :]
    for d in range(4):
        left = jnp.concatenate([rows_v[pl.ds(row_at[2 * d + i], BLK), :] for i in range(2)], axis=0)
        product = lax.dot_general(left, pick_v[...], DEPTH, preferred_element_type=jnp.float32)
        for e in range(4):
            for i in range(2):
                for j in range(2):
                    b = 2 * e + j
                    value = packed[(2 * d + i) * 8 + b].astype(jnp.float32)
                    value = value - product[i * BLK : (i + 1) * BLK, b * BLK : (b + 1) * BLK]
                    if d < 3:
                        ref, at = outs[d], (e * 2 + i) * 2 + j
                    else:
                        ref, at = outs[3 + e], i * 2 + j
                    ref[at * BLK : (at + 1) * BLK, :] = value.astype(jnp.bfloat16)


def picked(idx, shards, packed):
    size, depth = shards[0].shape
    return pl.pallas_call(
        picked_kernel,
        out_shape=[jax.ShapeDtypeStruct((blocks * BLK, BLK), jnp.bfloat16) for blocks in (16, 16, 16, 4, 4, 4, 4)],
        in_specs=[SMEM] + [VMEM] * 14,
        out_specs=[VMEM] * 7,
        scratch_shapes=[
            pltpu.VMEM((4 * size, depth), jnp.bfloat16),
            pltpu.VMEM((4 * size, depth), jnp.bfloat16),
            pltpu.VMEM((8 * BLK, depth), jnp.bfloat16),
        ],
        compiler_params=params(24),
        cost_estimate=pl.CostEstimate(flops=2 * 1024 * 1024 * 384, bytes_accessed=8 << 20, transcendentals=0),
        name="picked",
    )(idx, *shards, packed)


def update_kernel(idx, frontal, *refs):
    shards, out, owns = refs[:13], refs[13], refs[14:18]
    rows_v, cols_v, whole_v = refs[18:]
    step = pl.program_id(0)

    @pl.when(step == 0)
    def _():
        load_factor(shards, rows_v, cols_v)

    high = out.shape[0]
    left = rows_v[pl.ds(pl.multiple_of(step * high, high), high), :]
    product = lax.dot_general(left, cols_v[...], DEPTH, preferred_element_type=jnp.float32)
    value = frontal[...].astype(jnp.float32) - product
    out[...] = value.astype(jnp.bfloat16)
    whole_v[...] = value
    per = high // BLK
    for d in range(4):
        for i in range(2):
            at = idx[16 + 2 * d + i]

            @pl.when(at // per == step)
            def _():
                strip = pl.ds(pl.multiple_of(lax.rem(at, per) * BLK, BLK), BLK)
                for e in range(4):
                    for j in range(2):
                        k = ((e * 2 + i) * 2 + j) * BLK
                        wide = pl.ds(pl.multiple_of(idx[24 + 2 * e + j] * BLK, BLK), BLK)
                        owns[d][k : k + BLK, :] = whole_v[strip, wide]


def updated(idx, shards, frontal):
    tile, depth = frontal.shape[0], shards[0].shape[1]
    high = 512
    block = pl.BlockSpec((high, tile), lambda s: (s, 0))
    return pl.pallas_call(
        update_kernel,
        out_shape=[jax.ShapeDtypeStruct((tile, tile), jnp.bfloat16)]
        + [jax.ShapeDtypeStruct((16 * BLK, BLK), jnp.float32)] * 4,
        grid=(tile // high,),
        in_specs=[SMEM, block] + [VMEM] * 13,
        out_specs=[block] + [VMEM] * 4,
        scratch_shapes=[
            pltpu.VMEM((tile, depth), jnp.bfloat16),
            pltpu.VMEM((tile, depth), jnp.bfloat16),
            pltpu.VMEM((high, tile), jnp.float32),
        ],
        compiler_params=params(40),
        cost_estimate=pl.CostEstimate(flops=2 * tile * tile * depth, bytes_accessed=24 << 20, transcendentals=0),
        name="update",
    )(idx, frontal, *shards)


def place_kernel(first, split, idx, *refs):
    count = len(split)
    owns, parts = refs[:count], list(refs[count : count + sum(split)])
    out, block_v, sem = refs[-3:]
    for n in range(count):
        mine, parts = parts[: split[n]], parts[split[n] :]
        for e in range(4):
            for i in range(2):
                for j in range(2):
                    k = (e * 2 + i) * 2 + j
                    ref, at = (mine[0], k) if split[n] == 1 else (mine[e], i * 2 + j)
                    if e > 0 and ref.shape[0] == 8 * BLK:
                        at += n * 4
                    value = owns[n][k * BLK : (k + 1) * BLK, :]
                    value = value + ref[at * BLK : (at + 1) * BLK, :].astype(jnp.float32)
                    block_v[n * 16 + k] = value.astype(jnp.bfloat16)
                    pltpu.make_async_copy(
                        block_v.at[n * 16 + k],
                        out.at[
                            pl.ds(pl.multiple_of(idx[16 + 2 * (first + n) + i] * BLK, BLK), BLK),
                            pl.ds(pl.multiple_of(idx[24 + 2 * e + j] * BLK, BLK), BLK),
                        ],
                        sem,
                    ).start()
    pltpu.make_async_copy(block_v, block_v, sem).wait()


def placed(idx, first, own, parts, out):
    count = len(own)
    arrays = [array for piece in parts for array in piece]
    return pl.pallas_call(
        functools.partial(place_kernel, first, [len(piece) for piece in parts]),
        out_shape=jax.ShapeDtypeStruct(out.shape, out.dtype),
        in_specs=[SMEM] + [VMEM] * (count + len(arrays)) + [ANY],
        out_specs=ANY,
        scratch_shapes=[pltpu.VMEM((16 * count, BLK, BLK), jnp.bfloat16), pltpu.SemaphoreType.DMA],
        input_output_aliases={count + len(arrays) + 1: 0},
        compiler_params=params(12),
        cost_estimate=pl.CostEstimate(flops=1 << 18, bytes_accessed=count << 21, transcendentals=0),
        name="place",
    )(idx, *own, *arrays, out)


def after(array, *done):
    return lax.optimization_barrier((array, *done))[0]


def on_device(frontal, panel_cols, inv_factor, child_map, child_mask):
    front = frontal[0]
    quarter = 4 * BLK

    def hop(d, array):
        return move(array, lambda g, r, c: (g - 1, r ^ d, c))

    def flip_row(d, array):
        return move(array, lambda g, r, c: (g, r ^ d, c))

    def flip_col(d, array):
        return move(array, lambda g, r, c: (g, r, c ^ d))

    factor = lax.dot_general(panel_cols[0], inv_factor[0], DEPTH, preferred_element_type=jnp.float32).astype(
        jnp.bfloat16
    )
    across = flip_row(2, factor)
    near = [flip_col(1, factor), flip_col(3, factor)]
    idx = plan(child_map, child_mask)
    packed = pack(idx, front)
    row, col = lax.axis_index("row"), lax.axis_index("col")
    same = row // 2 == col // 2
    alike = (row + col) % 2 == 0
    across = after(across, idx)
    low, high = jnp.where(same, factor, across), jnp.where(same, across, factor)
    half = factor.shape[0] // 2
    by_col = [factor, *near, flip_col(1, near[1][:half]), flip_col(3, near[0][half:])]
    third = move(high, lambda g, r, c: (g, r, c ^ 3) if (r + c) % 2 else None)
    one = move(
        jnp.where(alike, high, low), lambda g, r, c: (g, r ^ 1, c ^ 1) if (r + c) % 2 else (g, r, c ^ 2)
    )

    def swap(array):
        return move(array, lambda g, r, c: None if (r + c) % 2 else (g, r ^ 1, c))

    other = flip_row(1, after(one, *by_col[3:]))
    shards = by_col + [low, swap(after(low, packed)), other, one, one, other, third, swap(after(third, *by_col[3:]))]
    sent = picked(idx, shards, packed)
    came = [hop(d, sent[d]) for d in range(3)]
    crossed = [sent[3]] + [flip_col(e, sent[3 + e]) for e in (1, 2, 3)]
    came.append(hop(3, jnp.concatenate(crossed)))
    out, *own = updated(idx, shards, after(front, came[0]))
    others = []
    for changes in ((0, 1), (2,)):
        others.append([])
        for e in (1, 2, 3):
            blocks = [came[d][e * quarter : (e + 1) * quarter] for d in changes]
            blocks = jnp.concatenate(blocks) if len(blocks) > 1 else blocks[0]
            others[-1].append(flip_col(e, after(blocks, own[0])))
    parts = [[came[0], *others[0]], [came[1], *others[0]], [came[2], *others[1]], [came[3]]]
    out = placed(idx, 0, own[:2], parts[:2], out)
    return placed(idx, 2, own[2:], parts[2:], out)[None]


def solution(mesh):
    specs = (
        P("group", "row", "col"),
        P("group", ("row", "col"), None),
        P("group", None, None),
        P(),
        P(),
    )
    return jax.shard_map(
        on_device, mesh=mesh, in_specs=specs, out_specs=P("group", "row", "col"), check_vma=False
    )
```

```python
import functools

import jax
import jax.numpy as jnp
from jax import lax
from jax.experimental import pallas as pl
from jax.experimental.pallas import tpu as pltpu
from jax.sharding import PartitionSpec as P

BLK = 128
AXES = ("group", "row", "col")
ANY = pl.BlockSpec(memory_space=pl.ANY)
SMEM = pl.BlockSpec(memory_space=pltpu.SMEM)
VMEM = pl.BlockSpec(memory_space=pltpu.VMEM)
DEPTH = (((1,), (1,)), ((), ()))


def params(mib):
    return pltpu.CompilerParams(vmem_limit_bytes=mib << 20)


def move(array, target):
    groups, rows, cols = (lax.axis_size(axis) for axis in AXES)
    pairs = []
    for g in range(groups):
        for r in range(rows):
            for c in range(cols):
                to = target(g, r, c)
                if to is not None and to[0] >= 0:
                    tg, tr, tc = to
                    pairs.append(((g * rows + r) * cols + c, (tg * rows + tr) * cols + tc))
    return lax.ppermute(array, AXES, pairs)


def codes(map_ref, mask_ref, group, run, span):
    out = []
    for k in range(span):
        target = map_ref[group, run * span + k]
        live = mask_ref[group, run * span + k] == 1
        out.append((jnp.where(live, target // span, -1), target * span + k))
    return out


def ends(coded, run):
    low, high = jnp.int32(1 << 20), jnp.int32(-1)
    for to, code in coded:
        hit = to == run
        low = jnp.minimum(low, jnp.where(hit, code, 1 << 20))
        high = jnp.maximum(high, jnp.where(hit, code, -1))
    return low, high


def plan_kernel(map_ref, mask_ref, out_ref):
    count = map_ref.shape[1]
    runs = lax.axis_size("row")
    span = count // runs
    group = lax.axis_index("group")
    child = jnp.minimum(group + 1, map_ref.shape[0] - 1)
    for position, axis in enumerate(("row", "col")):
        me = lax.axis_index(axis)
        own = codes(map_ref, mask_ref, group, me, span)
        for run in range(runs):
            for i, code in enumerate(ends(own, run)):
                out_ref[position * 2 * runs + 2 * run + i] = lax.rem(code, span)
        for d in range(runs):
            for i, code in enumerate(ends(codes(map_ref, mask_ref, child, me ^ d, span), me)):
                out_ref[(position + 2) * 2 * runs + 2 * d + i] = code // span - me * span


def plan(child_map, child_mask):
    return pl.pallas_call(
        plan_kernel,
        out_shape=jax.ShapeDtypeStruct((32,), jnp.int32),
        in_specs=[SMEM, SMEM],
        out_specs=SMEM,
        compiler_params=params(16),
        name="plan",
    )(child_map, child_mask)


def load_factor(shards, rows_v, cols_v):
    size = shards[0].shape[0]
    half = size // 2
    row, col = lax.axis_index("row"), lax.axis_index("col")
    alike = lax.rem(row + col, 2) == 0
    places = [((col ^ d) * size, size) for d in (0, 1, 3)] + [((col ^ 2) * size + n * half, half) for n in range(2)]
    for ref, (start, count) in zip(shards[:5], places):
        rows_v[pl.ds(pl.multiple_of(start, half), count), :] = ref[...]
    for d in range(4):
        place = pl.ds(pl.multiple_of((col ^ d) * size, size), size)

        @pl.when(alike)
        def _():
            cols_v[place, :] = shards[5 + 2 * d][...]

        @pl.when(jnp.logical_not(alike))
        def _():
            cols_v[place, :] = shards[6 + 2 * d][...]


def pack_kernel(idx, frontal, out, sem):
    row, col = lax.axis_index("row"), lax.axis_index("col")
    row_at = [pl.multiple_of(idx[2 * (row ^ d) + i] * BLK, BLK) for d in range(4) for i in range(2)]
    col_at = [pl.multiple_of(idx[8 + 2 * (col ^ e) + j] * BLK, BLK) for e in range(4) for j in range(2)]
    for a in range(8):
        for b in range(8):
            pltpu.make_async_copy(
                frontal.at[pl.ds(row_at[a], BLK), pl.ds(col_at[b], BLK)], out.at[a * 8 + b], sem
            ).start()
    pltpu.make_async_copy(out, out, sem).wait()


def pack(idx, frontal):
    return pl.pallas_call(
        pack_kernel,
        out_shape=jax.ShapeDtypeStruct((64, BLK, BLK), frontal.dtype),
        in_specs=[SMEM, ANY],
        out_specs=VMEM,
        scratch_shapes=[pltpu.SemaphoreType.DMA],
        compiler_params=params(16),
        cost_estimate=pl.CostEstimate(flops=0, bytes_accessed=4 << 20, transcendentals=0),
        name="pack",
    )(idx, frontal)


def picked_kernel(changes, idx, *refs):
    shards, packed = refs[:13], refs[13]
    outs = refs[14:-3]
    rows_v, cols_v, pick_v = refs[-3:]
    row, col = lax.axis_index("row"), lax.axis_index("col")
    load_factor(shards, rows_v, cols_v)
    row_at = [pl.multiple_of(idx[2 * (row ^ d) + i] * BLK, BLK) for d in range(4) for i in range(2)]
    col_at = [pl.multiple_of(idx[8 + 2 * (col ^ e) + j] * BLK, BLK) for e in range(4) for j in range(2)]
    for b in range(8):
        pick_v[b * BLK : (b + 1) * BLK, :] = cols_v[pl.ds(col_at[b], BLK), :]
    for d in changes:
        left = jnp.concatenate([rows_v[pl.ds(row_at[2 * d + i], BLK), :] for i in range(2)], axis=0)
        product = lax.dot_general(left, pick_v[...], DEPTH, preferred_element_type=jnp.float32)
        for e in range(4):
            for i in range(2):
                for j in range(2):
                    b = 2 * e + j
                    value = packed[(2 * d + i) * 8 + b].astype(jnp.float32)
                    value = value - product[i * BLK : (i + 1) * BLK, b * BLK : (b + 1) * BLK]
                    if d < 3:
                        ref, at = outs[d - changes[0]], (e * 2 + i) * 2 + j
                    else:
                        ref, at = outs[3 - changes[0] + e], i * 2 + j
                    ref[at * BLK : (at + 1) * BLK, :] = value.astype(jnp.bfloat16)


def picked(changes, idx, shards, packed):
    shard, depth = shards[0].shape
    sizes = [size for d in changes for size in ((16,) if d < 3 else (4,) * 4)]
    return pl.pallas_call(
        functools.partial(picked_kernel, changes),
        out_shape=[jax.ShapeDtypeStruct((blocks * BLK, BLK), jnp.bfloat16) for blocks in sizes],
        in_specs=[SMEM] + [VMEM] * 14,
        out_specs=[VMEM] * len(sizes),
        scratch_shapes=[
            pltpu.VMEM((4 * shard, depth), jnp.bfloat16),
            pltpu.VMEM((4 * shard, depth), jnp.bfloat16),
            pltpu.VMEM((8 * BLK, depth), jnp.bfloat16),
        ],
        compiler_params=params(24),
        cost_estimate=pl.CostEstimate(flops=2 * 1024 * 1024 * 384, bytes_accessed=8 << 20, transcendentals=0),
        name="picked",
    )(idx, *shards, packed)


def update_kernel(idx, frontal, *refs):
    shards, out, owns = refs[:13], refs[13], refs[14:18]
    rows_v, cols_v, whole_v = refs[18:]
    step = pl.program_id(0)

    @pl.when(step == 0)
    def _():
        load_factor(shards, rows_v, cols_v)

    high = out.shape[0]
    left = rows_v[pl.ds(pl.multiple_of(step * high, high), high), :]
    product = lax.dot_general(left, cols_v[...], DEPTH, preferred_element_type=jnp.float32)
    value = frontal[...].astype(jnp.float32) - product
    out[...] = value.astype(jnp.bfloat16)
    whole_v[...] = value
    per = high // BLK
    for d in range(4):
        for i in range(2):
            at = idx[16 + 2 * d + i]

            @pl.when(at // per == step)
            def _():
                strip = pl.ds(pl.multiple_of(lax.rem(at, per) * BLK, BLK), BLK)
                for e in range(4):
                    for j in range(2):
                        k = ((e * 2 + i) * 2 + j) * BLK
                        wide = pl.ds(pl.multiple_of(idx[24 + 2 * e + j] * BLK, BLK), BLK)
                        owns[d][k : k + BLK, :] = whole_v[strip, wide]


def updated(idx, shards, frontal):
    tile, depth = frontal.shape[0], shards[0].shape[1]
    high = 512
    block = pl.BlockSpec((high, tile), lambda s: (s, 0))
    return pl.pallas_call(
        update_kernel,
        out_shape=[jax.ShapeDtypeStruct((tile, tile), jnp.bfloat16)]
        + [jax.ShapeDtypeStruct((16 * BLK, BLK), jnp.float32)] * 4,
        grid=(tile // high,),
        in_specs=[SMEM, block] + [VMEM] * 13,
        out_specs=[block] + [VMEM] * 4,
        scratch_shapes=[
            pltpu.VMEM((tile, depth), jnp.bfloat16),
            pltpu.VMEM((tile, depth), jnp.bfloat16),
            pltpu.VMEM((high, tile), jnp.float32),
        ],
        compiler_params=params(40),
        cost_estimate=pl.CostEstimate(flops=2 * tile * tile * depth, bytes_accessed=24 << 20, transcendentals=0),
        name="update",
    )(idx, frontal, *shards)


def place_kernel(first, split, idx, *refs):
    count = len(split)
    owns, parts = refs[:count], list(refs[count : count + sum(split)])
    out, block_v, sem = refs[-3:]
    for n in range(count):
        mine, parts = parts[: split[n]], parts[split[n] :]
        for e in range(4):
            for i in range(2):
                for j in range(2):
                    k = (e * 2 + i) * 2 + j
                    ref, at = (mine[0], k) if split[n] == 1 else (mine[e], i * 2 + j)
                    if e > 0 and ref.shape[0] == 8 * BLK:
                        at += n * 4
                    value = owns[n][k * BLK : (k + 1) * BLK, :]
                    value = value + ref[at * BLK : (at + 1) * BLK, :].astype(jnp.float32)
                    block_v[n * 16 + k] = value.astype(jnp.bfloat16)
                    pltpu.make_async_copy(
                        block_v.at[n * 16 + k],
                        out.at[
                            pl.ds(pl.multiple_of(idx[16 + 2 * (first + n) + i] * BLK, BLK), BLK),
                            pl.ds(pl.multiple_of(idx[24 + 2 * e + j] * BLK, BLK), BLK),
                        ],
                        sem,
                    ).start()
    pltpu.make_async_copy(block_v, block_v, sem).wait()


def placed(idx, first, own, parts, out):
    count = len(own)
    arrays = [array for piece in parts for array in piece]
    return pl.pallas_call(
        functools.partial(place_kernel, first, [len(piece) for piece in parts]),
        out_shape=jax.ShapeDtypeStruct(out.shape, out.dtype),
        in_specs=[SMEM] + [VMEM] * (count + len(arrays)) + [ANY],
        out_specs=ANY,
        scratch_shapes=[pltpu.VMEM((16 * count, BLK, BLK), jnp.bfloat16), pltpu.SemaphoreType.DMA],
        input_output_aliases={count + len(arrays) + 1: 0},
        compiler_params=params(12),
        cost_estimate=pl.CostEstimate(flops=1 << 18, bytes_accessed=count << 21, transcendentals=0),
        name="place",
    )(idx, *own, *arrays, out)


def after(array, *done):
    return lax.optimization_barrier((array, *done))[0]


def on_device(frontal, panel_cols, inv_factor, child_map, child_mask):
    front = frontal[0]
    quarter = 4 * BLK

    def hop(d, array):
        return move(array, lambda g, r, c: (g - 1, r ^ d, c))

    def flip_row(d, array):
        return move(array, lambda g, r, c: (g, r ^ d, c))

    def flip_col(d, array):
        return move(array, lambda g, r, c: (g, r, c ^ d))

    factor = lax.dot_general(panel_cols[0], inv_factor[0], DEPTH, preferred_element_type=jnp.float32).astype(
        jnp.bfloat16
    )
    across = flip_row(2, factor)
    near = [flip_col(1, factor), flip_col(3, factor)]
    idx = plan(child_map, child_mask)
    packed = pack(idx, front)
    row, col = lax.axis_index("row"), lax.axis_index("col")
    same = row // 2 == col // 2
    alike = (row + col) % 2 == 0
    across = after(across, idx)
    low, high = jnp.where(same, factor, across), jnp.where(same, across, factor)
    half = factor.shape[0] // 2
    by_col = [factor, *near, flip_col(1, near[1][:half]), flip_col(3, near[0][half:])]
    third = move(high, lambda g, r, c: (g, r, c ^ 3) if (r + c) % 2 else None)
    one = move(
        jnp.where(alike, high, low), lambda g, r, c: (g, r ^ 1, c ^ 1) if (r + c) % 2 else (g, r, c ^ 2)
    )

    def swap(array):
        return move(array, lambda g, r, c: None if (r + c) % 2 else (g, r ^ 1, c))

    other = flip_row(1, after(one, *by_col[3:]))
    shards = by_col + [low, swap(after(low, packed)), other, one, one, other, third, swap(after(third, *by_col[3:]))]
    sent = picked((0,), idx, shards, packed)
    sent += picked((1, 2, 3), idx, shards, after(packed, sent[0]))
    came = [hop(d, sent[d]) for d in range(3)]
    crossed = [sent[3]] + [flip_col(e, sent[3 + e]) for e in (1, 2, 3)]
    came.append(hop(3, jnp.concatenate(crossed)))
    out, *own = updated(idx, shards, after(front, came[0]))
    others = []
    for changes in ((0, 1), (2,)):
        others.append([])
        for e in (1, 2, 3):
            blocks = [came[d][e * quarter : (e + 1) * quarter] for d in changes]
            blocks = jnp.concatenate(blocks) if len(blocks) > 1 else blocks[0]
            others[-1].append(flip_col(e, after(blocks, own[0])))
    parts = [[came[0], *others[0]], [came[1], *others[0]], [came[2], *others[1]], [came[3]]]
    out = placed(idx, 0, own[:2], parts[:2], out)
    return placed(idx, 2, own[2:], parts[2:], out)[None]


def solution(mesh):
    specs = (
        P("group", "row", "col"),
        P("group", ("row", "col"), None),
        P("group", None, None),
        P(),
        P(),
    )
    return jax.shard_map(
        on_device, mesh=mesh, in_specs=specs, out_specs=P("group", "row", "col"), check_vma=False
    )
```

```python
import functools

import jax
import jax.numpy as jnp
from jax import lax
from jax.experimental import pallas as pl
from jax.experimental.pallas import tpu as pltpu
from jax.sharding import PartitionSpec as P

BLK = 128
AXES = ("group", "row", "col")
ANY = pl.BlockSpec(memory_space=pl.ANY)
SMEM = pl.BlockSpec(memory_space=pltpu.SMEM)
VMEM = pl.BlockSpec(memory_space=pltpu.VMEM)
DEPTH = (((1,), (1,)), ((), ()))


def params(mib):
    return pltpu.CompilerParams(vmem_limit_bytes=mib << 20)


def move(array, target):
    groups, rows, cols = (lax.axis_size(axis) for axis in AXES)
    pairs = []
    for g in range(groups):
        for r in range(rows):
            for c in range(cols):
                to = target(g, r, c)
                if to is not None and to[0] >= 0:
                    tg, tr, tc = to
                    pairs.append(((g * rows + r) * cols + c, (tg * rows + tr) * cols + tc))
    return lax.ppermute(array, AXES, pairs)


def codes(map_ref, mask_ref, group, run, span):
    out = []
    for k in range(span):
        target = map_ref[group, run * span + k]
        live = mask_ref[group, run * span + k] == 1
        out.append((jnp.where(live, target // span, -1), target * span + k))
    return out


def ends(coded, run):
    low, high = jnp.int32(1 << 20), jnp.int32(-1)
    for to, code in coded:
        hit = to == run
        low = jnp.minimum(low, jnp.where(hit, code, 1 << 20))
        high = jnp.maximum(high, jnp.where(hit, code, -1))
    return low, high


def plan_kernel(map_ref, mask_ref, out_ref):
    count = map_ref.shape[1]
    runs = lax.axis_size("row")
    span = count // runs
    group = lax.axis_index("group")
    child = jnp.minimum(group + 1, map_ref.shape[0] - 1)
    for position, axis in enumerate(("row", "col")):
        me = lax.axis_index(axis)
        own = codes(map_ref, mask_ref, group, me, span)
        for run in range(runs):
            for i, code in enumerate(ends(own, run)):
                out_ref[position * 2 * runs + 2 * run + i] = lax.rem(code, span)
        for d in range(runs):
            for i, code in enumerate(ends(codes(map_ref, mask_ref, child, me ^ d, span), me)):
                out_ref[(position + 2) * 2 * runs + 2 * d + i] = code // span - me * span


def plan(child_map, child_mask):
    return pl.pallas_call(
        plan_kernel,
        out_shape=jax.ShapeDtypeStruct((32,), jnp.int32),
        in_specs=[SMEM, SMEM],
        out_specs=SMEM,
        compiler_params=params(16),
        name="plan",
    )(child_map, child_mask)


def load_factor(shards, rows_v, cols_v):
    size = shards[0].shape[0]
    half = size // 2
    row, col = lax.axis_index("row"), lax.axis_index("col")
    alike = lax.rem(row + col, 2) == 0
    places = [((col ^ d) * size, size) for d in (0, 1, 3)] + [((col ^ 2) * size + n * half, half) for n in range(2)]
    for ref, (start, count) in zip(shards[:5], places):
        rows_v[pl.ds(pl.multiple_of(start, half), count), :] = ref[...]
    for d in range(4):
        place = pl.ds(pl.multiple_of((col ^ d) * size, size), size)

        @pl.when(alike)
        def _():
            cols_v[place, :] = shards[5 + 2 * d][...]

        @pl.when(jnp.logical_not(alike))
        def _():
            cols_v[place, :] = shards[6 + 2 * d][...]


def pack_kernel(idx, frontal, out, sem):
    row, col = lax.axis_index("row"), lax.axis_index("col")
    row_at = [pl.multiple_of(idx[2 * (row ^ d) + i] * BLK, BLK) for d in range(4) for i in range(2)]
    col_at = [pl.multiple_of(idx[8 + 2 * (col ^ e) + j] * BLK, BLK) for e in range(4) for j in range(2)]
    for a in range(8):
        for b in range(8):
            pltpu.make_async_copy(
                frontal.at[pl.ds(row_at[a], BLK), pl.ds(col_at[b], BLK)], out.at[a * 8 + b], sem
            ).start()
    pltpu.make_async_copy(out, out, sem).wait()


def pack(idx, frontal):
    return pl.pallas_call(
        pack_kernel,
        out_shape=jax.ShapeDtypeStruct((64, BLK, BLK), frontal.dtype),
        in_specs=[SMEM, ANY],
        out_specs=VMEM,
        scratch_shapes=[pltpu.SemaphoreType.DMA],
        compiler_params=params(16),
        cost_estimate=pl.CostEstimate(flops=0, bytes_accessed=4 << 20, transcendentals=0),
        name="pack",
    )(idx, frontal)


def picked_kernel(changes, idx, *refs):
    shards, packed = refs[:13], refs[13]
    outs = refs[14:-3]
    rows_v, cols_v, pick_v = refs[-3:]
    row, col = lax.axis_index("row"), lax.axis_index("col")
    load_factor(shards, rows_v, cols_v)
    row_at = [pl.multiple_of(idx[2 * (row ^ d) + i] * BLK, BLK) for d in range(4) for i in range(2)]
    col_at = [pl.multiple_of(idx[8 + 2 * (col ^ e) + j] * BLK, BLK) for e in range(4) for j in range(2)]
    for b in range(8):
        pick_v[b * BLK : (b + 1) * BLK, :] = cols_v[pl.ds(col_at[b], BLK), :]
    for d in changes:
        left = jnp.concatenate([rows_v[pl.ds(row_at[2 * d + i], BLK), :] for i in range(2)], axis=0)
        product = lax.dot_general(left, pick_v[...], DEPTH, preferred_element_type=jnp.float32)
        for e in range(4):
            for i in range(2):
                for j in range(2):
                    b = 2 * e + j
                    value = packed[(2 * d + i) * 8 + b].astype(jnp.float32)
                    value = value - product[i * BLK : (i + 1) * BLK, b * BLK : (b + 1) * BLK]
                    if d < 3:
                        ref, at = outs[d - changes[0]], (e * 2 + i) * 2 + j
                    else:
                        ref, at = outs[3 - changes[0] + e], i * 2 + j
                    ref[at * BLK : (at + 1) * BLK, :] = value.astype(jnp.bfloat16)


def picked(changes, idx, shards, packed):
    shard, depth = shards[0].shape
    sizes = [size for d in changes for size in ((16,) if d < 3 else (4,) * 4)]
    return pl.pallas_call(
        functools.partial(picked_kernel, changes),
        out_shape=[jax.ShapeDtypeStruct((blocks * BLK, BLK), jnp.bfloat16) for blocks in sizes],
        in_specs=[SMEM] + [VMEM] * 14,
        out_specs=[VMEM] * len(sizes),
        scratch_shapes=[
            pltpu.VMEM((4 * shard, depth), jnp.bfloat16),
            pltpu.VMEM((4 * shard, depth), jnp.bfloat16),
            pltpu.VMEM((8 * BLK, depth), jnp.bfloat16),
        ],
        compiler_params=params(24),
        cost_estimate=pl.CostEstimate(flops=2 * 1024 * 1024 * 384, bytes_accessed=8 << 20, transcendentals=0),
        name="picked",
    )(idx, *shards, packed)


def update_kernel(idx, frontal, *refs):
    shards, out, owns = refs[:13], refs[13], refs[14:18]
    rows_v, cols_v, whole_v = refs[18:]
    step = pl.program_id(0)

    @pl.when(step == 0)
    def _():
        load_factor(shards, rows_v, cols_v)

    high = out.shape[0]
    left = rows_v[pl.ds(pl.multiple_of(step * high, high), high), :]
    product = lax.dot_general(left, cols_v[...], DEPTH, preferred_element_type=jnp.float32)
    value = frontal[...].astype(jnp.float32) - product
    out[...] = value.astype(jnp.bfloat16)
    whole_v[...] = value
    per = high // BLK
    for d in range(4):
        for i in range(2):
            at = idx[16 + 2 * d + i]

            @pl.when(at // per == step)
            def _():
                strip = pl.ds(pl.multiple_of(lax.rem(at, per) * BLK, BLK), BLK)
                for e in range(4):
                    for j in range(2):
                        k = ((e * 2 + i) * 2 + j) * BLK
                        wide = pl.ds(pl.multiple_of(idx[24 + 2 * e + j] * BLK, BLK), BLK)
                        owns[d][k : k + BLK, :] = whole_v[strip, wide]


def updated(idx, shards, frontal):
    tile, depth = frontal.shape[0], shards[0].shape[1]
    high = 512
    block = pl.BlockSpec((high, tile), lambda s: (s, 0))
    return pl.pallas_call(
        update_kernel,
        out_shape=[jax.ShapeDtypeStruct((tile, tile), jnp.bfloat16)]
        + [jax.ShapeDtypeStruct((16 * BLK, BLK), jnp.float32)] * 4,
        grid=(tile // high,),
        in_specs=[SMEM, block] + [VMEM] * 13,
        out_specs=[block] + [VMEM] * 4,
        scratch_shapes=[
            pltpu.VMEM((tile, depth), jnp.bfloat16),
            pltpu.VMEM((tile, depth), jnp.bfloat16),
            pltpu.VMEM((high, tile), jnp.float32),
        ],
        compiler_params=params(40),
        cost_estimate=pl.CostEstimate(flops=2 * tile * tile * depth, bytes_accessed=24 << 20, transcendentals=0),
        name="update",
    )(idx, frontal, *shards)


def place_kernel(first, split, idx, *refs):
    count = len(split)
    owns, parts = refs[:count], list(refs[count : count + sum(split)])
    out, block_v, sem = refs[-3:]
    for n in range(count):
        mine, parts = parts[: split[n]], parts[split[n] :]
        for e in range(4):
            for i in range(2):
                for j in range(2):
                    k = (e * 2 + i) * 2 + j
                    ref, at = (mine[0], k) if split[n] == 1 else (mine[e], i * 2 + j)
                    if e > 0 and ref.shape[0] == 8 * BLK:
                        at += n * 4
                    value = owns[n][k * BLK : (k + 1) * BLK, :]
                    value = value + ref[at * BLK : (at + 1) * BLK, :].astype(jnp.float32)
                    block_v[n * 16 + k] = value.astype(jnp.bfloat16)
                    pltpu.make_async_copy(
                        block_v.at[n * 16 + k],
                        out.at[
                            pl.ds(pl.multiple_of(idx[16 + 2 * (first + n) + i] * BLK, BLK), BLK),
                            pl.ds(pl.multiple_of(idx[24 + 2 * e + j] * BLK, BLK), BLK),
                        ],
                        sem,
                    ).start()
    pltpu.make_async_copy(block_v, block_v, sem).wait()


def placed(idx, first, own, parts, out):
    count = len(own)
    arrays = [array for piece in parts for array in piece]
    return pl.pallas_call(
        functools.partial(place_kernel, first, [len(piece) for piece in parts]),
        out_shape=jax.ShapeDtypeStruct(out.shape, out.dtype),
        in_specs=[SMEM] + [VMEM] * (count + len(arrays)) + [ANY],
        out_specs=ANY,
        scratch_shapes=[pltpu.VMEM((16 * count, BLK, BLK), jnp.bfloat16), pltpu.SemaphoreType.DMA],
        input_output_aliases={count + len(arrays) + 1: 0},
        compiler_params=params(12),
        cost_estimate=pl.CostEstimate(flops=1 << 18, bytes_accessed=count << 21, transcendentals=0),
        name="place",
    )(idx, *own, *arrays, out)


def after(array, *done):
    return lax.optimization_barrier((array, *done))[0]


def on_device(frontal, panel_cols, inv_factor, child_map, child_mask):
    front = frontal[0]
    quarter = 4 * BLK

    def hop(d, array):
        return move(array, lambda g, r, c: (g - 1, r ^ d, c))

    def flip_row(d, array):
        return move(array, lambda g, r, c: (g, r ^ d, c))

    def flip_col(d, array):
        return move(array, lambda g, r, c: (g, r, c ^ d))

    factor = lax.dot_general(panel_cols[0], inv_factor[0], DEPTH, preferred_element_type=jnp.float32).astype(
        jnp.bfloat16
    )
    across = flip_row(2, factor)
    near = [flip_col(1, factor), flip_col(3, factor)]
    idx = plan(child_map, child_mask)
    packed = pack(idx, front)
    row, col = lax.axis_index("row"), lax.axis_index("col")
    same = row // 2 == col // 2
    alike = (row + col) % 2 == 0
    across = after(across, idx)
    low, high = jnp.where(same, factor, across), jnp.where(same, across, factor)
    half = factor.shape[0] // 2
    by_col = [factor, *near, flip_col(1, near[1][:half]), flip_col(3, near[0][half:])]
    third = move(high, lambda g, r, c: (g, r, c ^ 3) if (r + c) % 2 else None)
    one = move(
        jnp.where(alike, high, low), lambda g, r, c: (g, r ^ 1, c ^ 1) if (r + c) % 2 else (g, r, c ^ 2)
    )

    def swap(array):
        return move(array, lambda g, r, c: None if (r + c) % 2 else (g, r ^ 1, c))

    other = flip_row(1, after(one, *by_col[3:]))
    shards = by_col + [low, swap(after(low, packed)), other, one, one, other, third, swap(after(third, *by_col[3:]))]
    sent = picked((0,), idx, shards, packed)
    last = picked((3,), idx, shards, after(packed, sent[0]))
    sent += picked((1, 2), idx, shards, after(packed, last[0]))
    sent += last
    came = [hop(d, sent[d]) for d in range(3)]
    crossed = [sent[3]] + [flip_col(e, sent[3 + e]) for e in (1, 2, 3)]
    came.append(hop(3, jnp.concatenate(crossed)))
    out, *own = updated(idx, shards, after(front, came[0]))
    others = []
    for changes in ((0, 1), (2,)):
        others.append([])
        for e in (1, 2, 3):
            blocks = [came[d][e * quarter : (e + 1) * quarter] for d in changes]
            blocks = jnp.concatenate(blocks) if len(blocks) > 1 else blocks[0]
            others[-1].append(flip_col(e, after(blocks, own[0])))
    parts = [[came[0], *others[0]], [came[1], *others[0]], [came[2], *others[1]], [came[3]]]
    out = placed(idx, 0, own[:2], parts[:2], out)
    return placed(idx, 2, own[2:], parts[2:], out)[None]


def solution(mesh):
    specs = (
        P("group", "row", "col"),
        P("group", ("row", "col"), None),
        P("group", None, None),
        P(),
        P(),
    )
    return jax.shard_map(
        on_device, mesh=mesh, in_specs=specs, out_specs=P("group", "row", "col"), check_vma=False
    )
```
